32 devices in a mesh: dom: 8 (over z, y), agg: 4 (over x, core).
Axes of the slice: x: 2, y: 2, z: 4, core: 2. Of those that a mesh axis runs over, the one named last changes fastest.
Arguments:
- initial_guess: float32 [64, 262144], P(None, ('dom', 'agg')), may hold values from -6 to 6
- right_side: float32 [64, 262144], P(None, ('dom', 'agg')), may hold values from -6 to 6
- fine_tiles: bfloat16 [2048, 7, 128, 128], P(('dom', 'agg'))
- fine_smoother: bfloat16 [2048, 128, 128], P(('dom', 'agg'))
- fine_columns: int32 [2048, 7], P(('dom', 'agg')), may hold values from 0 to 71, as said below
- fine_sends: int32 [32, 8], P(('dom', 'agg')), may hold values from 0 to 63
- aggregate_map: int32 [262144], P(('dom', 'agg')), may hold values from 0 to 1023, as said below
- coarse_tiles: bfloat16 [256, 7, 128, 128], P('dom')
- coarse_smoother: bfloat16 [256, 128, 128], P('dom')
- coarse_columns: int32 [256, 7], P('dom'), may hold values from 0 to 39, as said below
- coarse_sends: int32 [8, 8], P('dom'), may hold values from 0 to 31
Outputs:
- smoothed: float32 [64, 262144], P(None, ('dom', 'agg'))
The draws below stay inside these ranges and needn't reach their ends.
Inputs may be any that keep to these rules, and one draw needn't show every extreme that they name: `fine_columns`: in row block r of partition q, entry 0 is r, entries 1 to 3 are below 64, the last 3 entries are 64 or more. `coarse_columns`: in row block r of a group, entry 0 is r, entries 1 to 3 are below 32, the last 3 entries are 32 or more. `aggregate_map`: within each partition every value names exactly 8 of its rows; the rows of fine blocks 8 * c to 8 * c + 7 name values from c * 128 to c * 128 + 127.
All inputs are finite; a program needn't handle non-finite values.
Results may differ from the reference program's by a relative error of at most 0.02.
Values may be sent and summed in bfloat16 or wider, within the bound.
A program may use at most 128 MiB of HBM per device.

```python
import math
import jax
import jax.numpy as jnp
from jax import lax

BS = 128
RHS = 64
RB = 64
NNZL = 4
NNZG = 3
S = 1
S2 = 1
AGGR = 8
NNZ = 7
CB = 8
G2 = 32
NG = 8
NG2 = 8
NROWS = 262144
N_DOM = 8
N_AGG = 4
DEVICES = 32


def noise_draw(key, shape):
    return jnp.clip(jax.random.normal(key, shape, jnp.float32), -4.0, 4.0)


def block_tiles(key, count):
    width = NNZL + NNZG
    noise = noise_draw(key, (count, width, BS, BS))
    leading = (jnp.arange(width) == 0)[None, :, None, None]
    spread = jnp.where(leading, 0.3, 0.5) / math.sqrt(BS)
    identity = jnp.eye(BS, dtype=jnp.float32)[None, None, :, :]
    return noise * spread + jnp.where(leading, 6.0, 0.0) * identity


def smoother_tiles(key, count):
    noise = noise_draw(key, (count, BS, BS))
    identity = jnp.eye(BS, dtype=jnp.float32)[None, :, :]
    return noise * (0.1 / math.sqrt(BS)) + identity / 6.0


def column_draw(key, count, local, ghost):
    near_key, far_key = jax.random.split(key)
    own = (jnp.arange(count, dtype=jnp.int32) % local)[:, None]
    near = jax.random.randint(near_key, (count, NNZL - 1), 0, local, dtype=jnp.int32)
    far = jax.random.randint(far_key, (count, NNZG), local, local + ghost, dtype=jnp.int32)
    return jnp.concatenate([own, near, far], axis=1).astype(jnp.int32)


def draw_fine_tiles(key, part):
    return block_tiles(key, DEVICES * RB).astype(jnp.bfloat16)


def draw_fine_smoother(key, part):
    return smoother_tiles(key, DEVICES * RB).astype(jnp.bfloat16)


def draw_fine_columns(key, part):
    return column_draw(key, DEVICES * RB, RB, NG)


def draw_aggregate_map(key, part):
    key = jax.random.fold_in(key, 5)
    keys = jax.random.split(key, DEVICES * CB)
    orders = jax.vmap(lambda single: jax.random.permutation(single, AGGR * BS))(keys).astype(jnp.int32)
    offsets = (jnp.arange(DEVICES * CB, dtype=jnp.int32) % CB * BS)[:, None]
    return (orders // AGGR + offsets).reshape(-1).astype(jnp.int32)


def draw_coarse_tiles(key, part):
    return block_tiles(key, DEVICES * CB).astype(jnp.bfloat16)


def draw_coarse_smoother(key, part):
    return smoother_tiles(key, DEVICES * CB).astype(jnp.bfloat16)


def draw_coarse_columns(key, part):
    return column_draw(key, DEVICES * CB, G2, NG2)


def set_ends(values, rng, smallest, largest):
    longest = values.shape.index(max(values.shape))
    spots = []
    for shift in (0, 1):
        where = [jax.random.randint(jax.random.fold_in(rng, axis), (), 0, length) for axis, length in enumerate(values.shape)]
        where[longest] = (where[longest] + shift) % values.shape[longest]
        spots.append(tuple(where))
    return values.at[spots[0]].set(smallest).at[spots[1]].set(largest)


def block_scale(rng, dims, pieces, smallest, high):
    level, own = 1.0, jax.random.fold_in(rng, 6)
    for dim, blocks in pieces:
        steps = jnp.exp(jax.random.uniform(jax.random.fold_in(own, dim), (blocks,), jnp.float32, smallest / len(pieces), high / len(pieces)))
        level = level * jnp.repeat(steps, dims[dim] // blocks).reshape([-1 if axis == dim else 1 for axis in range(len(dims))])
    return level


def gaussian(key, shape, deviation, reach, shards=(), kind=jnp.bfloat16):
    gain = block_scale(key, shape, shards, -0.22, 0.18) if shards else 1.0
    entries = jax.random.normal(key, shape, jnp.float32) * deviation * gain
    return jnp.minimum(jnp.maximum(entries, -reach), reach).astype(kind)


def setup_inputs(seed: int = 0) -> dict:
    seeds = jax.random.split(jax.random.key(seed), 12)
    initial_guess = gaussian(seeds[0], (RHS, NROWS), 1.0, 6.0, ((1, 32),), jnp.float32)
    right_side = gaussian(seeds[1], (RHS, NROWS), 1.0, 6.0, ((1, 32),), jnp.float32)
    fine_tiles = draw_fine_tiles(jax.random.fold_in(seeds[11], 71), 0)
    fine_smoother = draw_fine_smoother(jax.random.fold_in(seeds[11], 71), 0)
    fine_columns = draw_fine_columns(jax.random.fold_in(seeds[11], 71), 0)
    fine_sends = set_ends(jax.random.randint(seeds[5], (DEVICES, NG), 0, RB), jax.random.fold_in(seeds[5], 1), 0, RB - 1).astype(jnp.int32)
    aggregate_map = draw_aggregate_map(jax.random.fold_in(seeds[11], 71), 0)
    coarse_tiles = draw_coarse_tiles(jax.random.fold_in(seeds[11], 71), 0)
    coarse_smoother = draw_coarse_smoother(jax.random.fold_in(seeds[11], 71), 0)
    coarse_columns = draw_coarse_columns(jax.random.fold_in(seeds[11], 71), 0)
    coarse_sends = set_ends(jax.random.randint(seeds[10], (N_DOM, NG2), 0, G2), jax.random.fold_in(seeds[10], 1), 0, G2 - 1).astype(jnp.int32)
    return dict(initial_guess=initial_guess, right_side=right_side, fine_tiles=fine_tiles, fine_smoother=fine_smoother, fine_columns=fine_columns, fine_sends=fine_sends, aggregate_map=aggregate_map, coarse_tiles=coarse_tiles, coarse_smoother=coarse_smoother, coarse_columns=coarse_columns, coarse_sends=coarse_sends)


def ghost_blocks(blocks, sends, groups, members, slots):
    sent = jax.vmap(lambda part, picks: jnp.take(part, picks, axis=1), in_axes=(1, 0), out_axes=1)(blocks, sends)
    count = sent.shape[0]
    sent = sent.reshape(count, groups, members, groups, slots, BS)
    sent = jnp.transpose(sent, (0, 3, 2, 1, 4, 5))
    return sent.reshape(count, groups * members, groups * slots, BS)


def apply_blocks(extended, tiles, columns):
    parts = extended.shape[1]
    tiles = tiles.reshape(parts, -1, NNZ, BS, BS)
    columns = columns.reshape(parts, -1, NNZ)

    def per_part(items):
        ext_blocks, part_tiles, part_columns = items
        operand = jnp.take(ext_blocks, part_columns, axis=1)
        return jnp.einsum('hrkb,rkbc->hrc', operand.astype(jnp.float32), part_tiles.astype(jnp.float32))

    result = lax.map(per_part, (jnp.moveaxis(extended, 1, 0), tiles, columns))
    return jnp.moveaxis(result, 0, 1)


def smooth(values, smoother, parts):
    blocks = smoother.reshape(parts, -1, BS, BS)
    return jnp.einsum('hprb,prbc->hprc', values.astype(jnp.float32), blocks.astype(jnp.float32))


def reference(initial_guess, right_side, fine_tiles, fine_smoother, fine_columns, fine_sends, aggregate_map, coarse_tiles, coarse_smoother, coarse_columns, coarse_sends):
    shape_four = (RHS, DEVICES, RB, BS)
    iterate = initial_guess.reshape(shape_four)
    source = right_side.reshape(shape_four)

    def residual(current):
        rounded = current.astype(jnp.bfloat16)
        ghosts = ghost_blocks(rounded, fine_sends, N_DOM, N_AGG, S)
        extended = jnp.concatenate([rounded, ghosts], axis=2)
        return source - apply_blocks(extended, fine_tiles, fine_columns)

    def sweep(current):
        rounded = residual(current).astype(jnp.bfloat16)
        return current + smooth(rounded, fine_smoother, DEVICES)

    iterate = sweep(sweep(iterate))
    remain = residual(iterate).reshape(RHS, DEVICES, RB * BS)
    maps = aggregate_map.reshape(DEVICES, RB * BS)
    coarse = jax.vmap(lambda vals, idx: jnp.zeros((RHS, CB * BS), jnp.float32).at[:, idx].add(vals), in_axes=(1, 0), out_axes=1)(remain, maps)
    coarse_b = coarse.astype(jnp.bfloat16).reshape(RHS, N_DOM, G2, BS)
    first = smooth(coarse_b, coarse_smoother, N_DOM)
    first_b = first.astype(jnp.bfloat16)
    ghosts = ghost_blocks(first_b, coarse_sends, N_DOM, 1, S2)
    extended = jnp.concatenate([first_b, ghosts], axis=2)
    coarse_left = coarse_b.astype(jnp.float32) - apply_blocks(extended, coarse_tiles, coarse_columns)
    second = first + smooth(coarse_left.astype(jnp.bfloat16), coarse_smoother, N_DOM)
    second = second.reshape(RHS, DEVICES, CB * BS)
    lifted = jax.vmap(lambda vals, idx: jnp.take(vals, idx, axis=1), in_axes=(1, 0), out_axes=1)(second, maps)
    iterate = iterate + lifted.reshape(shape_four)
    iterate = sweep(sweep(iterate))
    return iterate.reshape(RHS, NROWS)
```

```python
import functools

import jax
import jax.numpy as jnp
from jax import lax
from jax.experimental import pallas as pl
from jax.experimental.pallas import tpu as pltpu
from jax.sharding import PartitionSpec as P

AGGR = 8
LOCAL = 4
BF = jnp.bfloat16
F32 = jnp.float32
MESH = pl.DeviceIdType.MESH
UNROLL = 8


def mm(a, b):
    return jnp.dot(a, b, preferred_element_type=F32)


def kernel(
    n,
    m,
    x_in,
    b_in,
    ft_in,
    fs_in,
    map_in,
    ct_in,
    cs_in,
    fc,
    fsend,
    cc,
    csend,
    out,
    stage,
    b,
    ft,
    fs,
    amap,
    ct,
    cs,
    x,
    xb,
    acc,
    member,
    send,
    ghost,
    e1,
    cb,
    e2,
    gath,
    lsem,
    tsem,
    ssem,
    rsem,
    gssem,
    grsem,
    osem,
):
    me = lax.axis_index("dom")
    ag = lax.axis_index("agg")
    own, systems, width = x.shape
    coarse = own // AGGR
    chunks = own // UNROLL
    split = LOCAL * width

    def lanes(r, count=1):
        return pl.ds(pl.multiple_of(r * width, width), count * width)

    load_x = pltpu.make_async_copy(x_in, stage, lsem.at[0])
    load_map = pltpu.make_async_copy(map_in, amap, lsem.at[1])
    load_b = pltpu.make_async_copy(b_in, b, lsem.at[2])
    load_fs = pltpu.make_async_copy(fs_in, fs, lsem.at[3])
    mine = pl.ds(ag * coarse, coarse)
    load_ct = pltpu.make_async_copy(ct_in.at[mine], ct, lsem.at[4])
    load_cs = pltpu.make_async_copy(cs_in.at[mine], cs, lsem.at[5])

    def load_tiles(c):
        rows = pl.ds(c * UNROLL, UNROLL)
        return pltpu.make_async_copy(ft_in.at[rows], ft.at[rows], tsem.at[c])

    load_x.start()
    load_map.start()
    load_b.start()
    for c in range(chunks):
        load_tiles(c).start()
    load_fs.start()
    load_ct.start()
    load_cs.start()

    barrier = pltpu.get_barrier_semaphore()
    for o in range(1, n):
        pl.semaphore_signal(
            barrier, inc=1, device_id=(lax.rem(me + o, n), ag), device_id_type=MESH
        )
    for o in range(1, m):
        pl.semaphore_signal(
            barrier, inc=1, device_id=(me, lax.rem(ag + o, m)), device_id_type=MESH
        )

    def exchange(e, table, rows_of):
        group = min(UNROLL, n)
        for first in range(1, n + 1, group):
            places = [lax.rem(me + o, n) for o in range(first, min(first + group, n + 1))]
            values = rows_of([table[0, d] for d in places])
            for i, (d, value) in enumerate(zip(places, values)):
                if first + i < n:
                    send[e, d] = value
                else:
                    ghost[e][d] = value
            for i, d in enumerate(places):
                if first + i < n:
                    pltpu.make_async_remote_copy(
                        src_ref=send.at[e, d],
                        dst_ref=ghost[e].at[me],
                        send_sem=ssem.at[e],
                        recv_sem=rsem.at[e],
                        device_id=(d, ag),
                        device_id_type=MESH,
                    ).start()

    def all_of(e):
        return pltpu.make_async_remote_copy(
            src_ref=send.at[e, pl.ds(0, n - 1)],
            dst_ref=ghost[e].at[pl.ds(0, n - 1)],
            send_sem=ssem.at[e],
            recv_sem=rsem.at[e],
            device_id=(lax.rem(me + 1, n), ag),
            device_id_type=MESH,
        )

    def ghost_part(e, r):
        near = ft.shape[1] // width
        parts = [ghost[e][jnp.maximum(fc[k, r] - own, 0)] for k in range(LOCAL, near)]
        return mm(jnp.concatenate(parts, axis=1), ft[r, split:, :])

    def local_phase(waits):
        @pl.loop(0, chunks)
        def _(c):
            if waits:
                load_tiles(c).wait()
            results = []
            for u in range(UNROLL):
                r = c * UNROLL + u
                parts = [xb[r]] + [xb[fc[k, r]] for k in range(1, LOCAL)]
                total = mm(jnp.concatenate(parts, axis=1), ft[r, :split, :])
                results.append(b[:, lanes(r)] - total)
            for u in range(UNROLL):
                acc[c * UNROLL + u] = results[u]

    def updated(e, rows):
        rest = [(acc[r] - ghost_part(e, r)).astype(BF) for r in rows]
        return [x[r] + mm(v, fs[r]) for r, v in zip(rows, rest)]

    def ghost_phase(e):
        @pl.loop(0, chunks)
        def _(c):
            rows = [c * UNROLL + u for u in range(UNROLL)]
            fresh = updated(e, rows)
            for r, v in zip(rows, fresh):
                x[r] = v
                xb[r] = v.astype(BF)

    def sweep(e, waits=False):
        local_phase(waits)
        if waits:
            load_fs.wait()
        all_of(e).wait_recv()
        exchange(e + 1, fsend, lambda rows: [v.astype(BF) for v in updated(e, rows)])
        ghost_phase(e)

    load_x.wait()

    @pl.loop(0, chunks)
    def _(c):
        for u in range(UNROLL):
            r = c * UNROLL + u
            v = stage[:, lanes(r)]
            x[r] = v
            xb[r] = v.astype(BF)

    pl.semaphore_wait(barrier, n - 1 + m - 1)
    exchange(0, fsend, lambda rows: [xb[r] for r in rows])

    load_map.wait()

    @pl.loop(0, own)
    def _(r):
        names = amap[pl.ds(r, 1), :] - (r // AGGR) * width
        wanted = lax.broadcasted_iota(jnp.int32, (width, width), 0)
        member[r] = jnp.where(names == wanted, 1.0, 0.0).astype(BF)

    load_b.wait()
    sweep(0, True)
    sweep(1)

    local_phase(False)
    load_ct.wait()
    load_cs.wait()
    all_of(2).wait_recv()

    @pl.loop(0, coarse)
    def _(c):
        rows = [c * AGGR + u for u in range(AGGR)]
        remain = [acc[r] - ghost_part(2, r) for r in rows]
        high = [v.astype(BF) for v in remain]
        low = [(v - h.astype(F32)).astype(BF) for v, h in zip(remain, high)]
        both = jnp.concatenate(
            [jnp.concatenate(high, axis=1), jnp.concatenate(low, axis=1)], axis=0
        )
        table = jnp.concatenate([member[r] for r in rows], axis=1)
        total = lax.dot_general(
            both, table, (((1,), (1,)), ((), ())), preferred_element_type=F32
        )
        kept = (total[:systems] + total[systems:]).astype(BF)
        cb[c] = kept
        first = mm(kept, cs[c])
        e1[c] = first
        gath[ag * coarse + c] = first.astype(BF)

    def gather_to(other, place):
        return pltpu.make_async_remote_copy(
            src_ref=gath.at[place],
            dst_ref=gath.at[place],
            send_sem=gssem.at[0],
            recv_sem=grsem.at[0],
            device_id=(me, other),
            device_id_type=MESH,
        )

    for o in range(1, m):
        gather_to(lax.rem(ag + o, m), mine).start()
    gather_all = gather_to(lax.rem(ag + 1, m), pl.ds(0, (m - 1) * coarse))
    gather_all.wait_recv()
    exchange(5, csend, lambda rows: [gath[r] for r in rows])
    left = []
    for j in range(coarse):
        r = ag * coarse + j
        parts = [gath[r]] + [gath[cc[k, r]] for k in range(1, LOCAL)]
        left.append(cb[j].astype(F32) - mm(jnp.concatenate(parts, axis=1), ct[j, :split, :]))
    for j in range(coarse):
        acc[j] = left[j]
    all_of(5).wait_recv()
    group = m * coarse
    rest = []
    for j in range(coarse):
        r = ag * coarse + j
        near = ct.shape[1] // width
        parts = [ghost[5][jnp.maximum(cc[k, r] - group, 0)] for k in range(LOCAL, near)]
        rest.append((acc[j] - mm(jnp.concatenate(parts, axis=1), ct[j, split:, :])).astype(BF))
    for j in range(coarse):
        second = e1[j] + mm(rest[j], cs[j])
        high = second.astype(BF)
        e2[j, :systems] = high
        e2[j, systems:] = (second - high.astype(F32)).astype(BF)

    def lifted(rows):
        both = [mm(e2[r // AGGR], member[r]) for r in rows]
        return [x[r] + (v[:systems] + v[systems:]) for r, v in zip(rows, both)]

    exchange(3, fsend, lambda rows: [v.astype(BF) for v in lifted(rows)])

    @pl.loop(0, chunks)
    def _(c):
        rows = [c * UNROLL + u for u in range(UNROLL)]
        fresh = lifted(rows)
        for r, v in zip(rows, fresh):
            x[r] = v
            xb[r] = v.astype(BF)

    sweep(3)
    local_phase(False)
    all_of(4).wait_recv()

    def store_out(c):
        place = lanes(c * UNROLL, UNROLL)
        return pltpu.make_async_copy(stage.at[:, place], out.at[:, place], osem.at[c])

    @pl.loop(0, chunks)
    def _(c):
        rows = [c * UNROLL + u for u in range(UNROLL)]
        fresh = updated(4, rows)
        for r, v in zip(rows, fresh):
            stage[:, lanes(r)] = v
        store_out(c).start()

    for e in range(6):
        all_of(e).wait_send()
    gather_all.wait_send()

    @pl.loop(0, chunks)
    def _(c):
        store_out(c).wait()


def shards(n, m, x, b, ft, fs, fc, fsend, amap, ct, cs, cc, csend):
    own, tiles, width, _ = ft.shape
    systems = x.shape[0]
    group = ct.shape[0]
    coarse = own // AGGR
    chunks = own // UNROLL
    hbm = pl.BlockSpec(memory_space=pl.ANY)
    smem = pl.BlockSpec(memory_space=pltpu.SMEM)
    block = (systems, width)
    return pl.pallas_call(
        functools.partial(kernel, n, m),
        out_shape=jax.ShapeDtypeStruct(x.shape, F32),
        in_specs=[hbm] * 7 + [smem] * 4,
        out_specs=hbm,
        scratch_shapes=[
            pltpu.VMEM(x.shape, F32),
            pltpu.VMEM(x.shape, F32),
            pltpu.VMEM((own, tiles * width, width), BF),
            pltpu.VMEM((own, width, width), BF),
            pltpu.VMEM((own, width), jnp.int32),
            pltpu.VMEM((coarse, tiles * width, width), BF),
            pltpu.VMEM((coarse, width, width), BF),
            pltpu.VMEM((own,) + block, F32),
            pltpu.VMEM((own,) + block, BF),
            pltpu.VMEM((own,) + block, F32),
            pltpu.VMEM((own, width, width), BF),
            pltpu.VMEM((6, n) + block, BF),
            [pltpu.VMEM((n,) + block, BF)] * 6,
            pltpu.VMEM((coarse,) + block, F32),
            pltpu.VMEM((coarse,) + block, BF),
            pltpu.VMEM((coarse, 2 * systems, width), BF),
            pltpu.VMEM((group,) + block, BF),
            pltpu.SemaphoreType.DMA((6,)),
            pltpu.SemaphoreType.DMA((chunks,)),
            pltpu.SemaphoreType.DMA((6,)),
            pltpu.SemaphoreType.DMA((6,)),
            pltpu.SemaphoreType.DMA((1,)),
            pltpu.SemaphoreType.DMA((1,)),
            pltpu.SemaphoreType.DMA((chunks,)),
        ],
        compiler_params=pltpu.CompilerParams(
            collective_id=0, has_side_effects=True, vmem_limit_bytes=60 * 1024 * 1024
        ),
        cost_estimate=pl.CostEstimate(
            flops=6_000_000_000, bytes_accessed=27_000_000, transcendentals=0
        ),
    )(
        x,
        b,
        ft.reshape(own, tiles * width, width),
        fs,
        amap.reshape(own, width),
        ct.reshape(group, tiles * width, width),
        cs,
        fc.T,
        fsend,
        cc.T,
        csend,
    )


def solution(mesh):
    return jax.shard_map(
        functools.partial(shards, mesh.shape["dom"], mesh.shape["agg"]),
        mesh=mesh,
        in_specs=(
            P(None, ("dom", "agg")),
            P(None, ("dom", "agg")),
            P(("dom", "agg"), None, None, None),
            P(("dom", "agg"), None, None),
            P(("dom", "agg"), None),
            P(("dom", "agg"), None),
            P(("dom", "agg")),
            P("dom", None, None, None),
            P("dom", None, None),
            P("dom", None),
            P("dom", None),
        ),
        out_specs=P(None, ("dom", "agg")),
        check_vma=False,
    )
```

```python
import functools

import jax
import jax.numpy as jnp
from jax import lax
from jax.experimental import pallas as pl
from jax.experimental.pallas import tpu as pltpu
from jax.sharding import PartitionSpec as P

AGGR = 8
LOCAL = 4
BF = jnp.bfloat16
F32 = jnp.float32
MESH = pl.DeviceIdType.MESH
UNROLL = 32
PIECE = 8


def mm(a, b):
    return jnp.dot(a, b, preferred_element_type=F32)


def kernel(
    n,
    m,
    x_in,
    b_in,
    ft_in,
    fs_in,
    map_in,
    ct_in,
    cs_in,
    fc,
    fsend,
    cc,
    csend,
    out,
    stage,
    b,
    ft,
    fs,
    amap,
    ct,
    cs,
    x,
    xb,
    acc,
    member,
    send,
    ghost,
    e1,
    cb,
    e2,
    gath,
    lsem,
    tsem,
    ssem,
    rsem,
    gssem,
    grsem,
    osem,
):
    me = lax.axis_index("dom")
    ag = lax.axis_index("agg")
    own, systems, width = x.shape
    coarse = own // AGGR
    chunks = own // UNROLL
    pieces = own // PIECE
    split = LOCAL * width

    def lanes(r, count=1):
        return pl.ds(pl.multiple_of(r * width, width), count * width)

    load_x = pltpu.make_async_copy(x_in, stage, lsem.at[0])
    load_map = pltpu.make_async_copy(map_in, amap, lsem.at[1])
    load_b = pltpu.make_async_copy(b_in, b, lsem.at[2])
    load_fs = pltpu.make_async_copy(fs_in, fs, lsem.at[3])
    mine = pl.ds(ag * coarse, coarse)
    load_ct = pltpu.make_async_copy(ct_in.at[mine], ct, lsem.at[4])
    load_cs = pltpu.make_async_copy(cs_in.at[mine], cs, lsem.at[5])

    def load_tiles(c):
        rows = pl.ds(c * PIECE, PIECE)
        return pltpu.make_async_copy(ft_in.at[rows], ft.at[rows], tsem.at[c])

    load_x.start()
    load_map.start()
    load_b.start()
    for c in range(pieces):
        load_tiles(c).start()
    load_fs.start()
    load_ct.start()
    load_cs.start()

    barrier = pltpu.get_barrier_semaphore()
    for o in range(1, n):
        pl.semaphore_signal(
            barrier, inc=1, device_id=(lax.rem(me + o, n), ag), device_id_type=MESH
        )
    for o in range(1, m):
        pl.semaphore_signal(
            barrier, inc=1, device_id=(me, lax.rem(ag + o, m)), device_id_type=MESH
        )

    def exchange(e, table, rows_of):
        group = min(PIECE, n)
        for first in range(1, n + 1, group):
            places = [lax.rem(me + o, n) for o in range(first, min(first + group, n + 1))]
            values = rows_of([table[0, d] for d in places])
            for i, (d, value) in enumerate(zip(places, values)):
                if first + i < n:
                    send[e, d] = value
                else:
                    ghost[e][d] = value
            for i, d in enumerate(places):
                if first + i < n:
                    pltpu.make_async_remote_copy(
                        src_ref=send.at[e, d],
                        dst_ref=ghost[e].at[me],
                        send_sem=ssem.at[e],
                        recv_sem=rsem.at[e],
                        device_id=(d, ag),
                        device_id_type=MESH,
                    ).start()

    def all_of(e):
        return pltpu.make_async_remote_copy(
            src_ref=send.at[e, pl.ds(0, n - 1)],
            dst_ref=ghost[e].at[pl.ds(0, n - 1)],
            send_sem=ssem.at[e],
            recv_sem=rsem.at[e],
            device_id=(lax.rem(me + 1, n), ag),
            device_id_type=MESH,
        )

    def ghost_part(e, r):
        near = ft.shape[1] // width
        parts = [ghost[e][jnp.maximum(fc[k, r] - own, 0)] for k in range(LOCAL, near)]
        return mm(jnp.concatenate(parts, axis=1), ft[r, split:, :])

    def local_phase(waits):
        size = PIECE if waits else UNROLL

        @pl.loop(0, own // size)
        def _(c):
            if waits:
                load_tiles(c).wait()
            for u in range(size):
                r = c * size + u
                parts = [xb[r]] + [xb[fc[k, r]] for k in range(1, LOCAL)]
                total = mm(jnp.concatenate(parts, axis=1), ft[r, :split, :])
                acc[r] = b[:, lanes(r)] - total

    def updated(e, rows):
        rest = [(acc[r] - ghost_part(e, r)).astype(BF) for r in rows]
        return [x[r] + mm(v, fs[r]) for r, v in zip(rows, rest)]

    def ghost_phase(e):
        @pl.loop(0, chunks)
        def _(c):
            rows = [c * UNROLL + u for u in range(UNROLL)]
            fresh = updated(e, rows)
            for r, v in zip(rows, fresh):
                x[r] = v
                xb[r] = v.astype(BF)

    def sweep(e, waits=False):
        local_phase(waits)
        if waits:
            load_fs.wait()
        all_of(e).wait_recv()
        exchange(e + 1, fsend, lambda rows: [v.astype(BF) for v in updated(e, rows)])
        ghost_phase(e)

    load_x.wait()

    @pl.loop(0, pieces)
    def _(c):
        for u in range(PIECE):
            r = c * PIECE + u
            v = stage[:, lanes(r)]
            x[r] = v
            xb[r] = v.astype(BF)

    pl.semaphore_wait(barrier, n - 1 + m - 1)
    exchange(0, fsend, lambda rows: [xb[r] for r in rows])

    load_map.wait()

    @pl.loop(0, own)
    def _(r):
        names = amap[pl.ds(r, 1), :] - (r // AGGR) * width
        wanted = lax.broadcasted_iota(jnp.int32, (width, width), 0)
        member[r] = jnp.where(names == wanted, 1.0, 0.0).astype(BF)

    load_b.wait()
    sweep(0, True)
    sweep(1)

    local_phase(False)
    load_ct.wait()
    load_cs.wait()
    all_of(2).wait_recv()

    @pl.loop(0, coarse)
    def _(c):
        rows = [c * AGGR + u for u in range(AGGR)]
        remain = [acc[r] - ghost_part(2, r) for r in rows]
        high = [v.astype(BF) for v in remain]
        low = [(v - h.astype(F32)).astype(BF) for v, h in zip(remain, high)]
        both = jnp.concatenate(
            [jnp.concatenate(high, axis=1), jnp.concatenate(low, axis=1)], axis=0
        )
        table = jnp.concatenate([member[r] for r in rows], axis=1)
        total = lax.dot_general(
            both, table, (((1,), (1,)), ((), ())), preferred_element_type=F32
        )
        kept = (total[:systems] + total[systems:]).astype(BF)
        cb[c] = kept
        first = mm(kept, cs[c])
        e1[c] = first
        gath[ag * coarse + c] = first.astype(BF)

    def slab(owner):
        return pl.ds(owner * coarse, coarse)

    def gather_to(other, owner, slot):
        return pltpu.make_async_remote_copy(
            src_ref=gath.at[slab(owner)],
            dst_ref=gath.at[slab(owner)],
            send_sem=gssem.at[slot],
            recv_sem=grsem.at[slot],
            device_id=(me, other),
            device_id_type=MESH,
        )

    mate = ag + 1 - 2 * lax.rem(ag, 2)
    far = lax.rem(ag + 2, 4)
    gathers = [gather_to(far, ag, 0), gather_to(mate, ag, 1), gather_to(mate, far, 2)]
    gathers[0].start()
    gathers[1].start()
    gathers[0].wait_recv()
    gathers[2].start()
    gathers[1].wait_recv()
    gathers[2].wait_recv()
    exchange(5, csend, lambda rows: [gath[r] for r in rows])
    left = []
    for j in range(coarse):
        r = ag * coarse + j
        parts = [gath[r]] + [gath[cc[k, r]] for k in range(1, LOCAL)]
        left.append(cb[j].astype(F32) - mm(jnp.concatenate(parts, axis=1), ct[j, :split, :]))
    for j in range(coarse):
        acc[j] = left[j]
    all_of(5).wait_recv()
    group = m * coarse
    rest = []
    for j in range(coarse):
        r = ag * coarse + j
        near = ct.shape[1] // width
        parts = [ghost[5][jnp.maximum(cc[k, r] - group, 0)] for k in range(LOCAL, near)]
        rest.append((acc[j] - mm(jnp.concatenate(parts, axis=1), ct[j, split:, :])).astype(BF))
    for j in range(coarse):
        second = e1[j] + mm(rest[j], cs[j])
        high = second.astype(BF)
        e2[j, :systems] = high
        e2[j, systems:] = (second - high.astype(F32)).astype(BF)

    def lifted(rows):
        both = [mm(e2[r // AGGR], member[r]) for r in rows]
        return [x[r] + (v[:systems] + v[systems:]) for r, v in zip(rows, both)]

    exchange(3, fsend, lambda rows: [v.astype(BF) for v in lifted(rows)])

    @pl.loop(0, chunks)
    def _(c):
        rows = [c * UNROLL + u for u in range(UNROLL)]
        fresh = lifted(rows)
        for r, v in zip(rows, fresh):
            x[r] = v
            xb[r] = v.astype(BF)

    sweep(3)
    local_phase(False)
    all_of(4).wait_recv()

    def store_out(c):
        place = lanes(c * UNROLL, UNROLL)
        return pltpu.make_async_copy(stage.at[:, place], out.at[:, place], osem.at[c])

    @pl.loop(0, chunks)
    def _(c):
        rows = [c * UNROLL + u for u in range(UNROLL)]
        fresh = updated(4, rows)
        for r, v in zip(rows, fresh):
            stage[:, lanes(r)] = v
        store_out(c).start()

    for e in range(6):
        all_of(e).wait_send()
    for copy in gathers:
        copy.wait_send()

    @pl.loop(0, chunks)
    def _(c):
        store_out(c).wait()


def shards(n, m, x, b, ft, fs, fc, fsend, amap, ct, cs, cc, csend):
    own, tiles, width, _ = ft.shape
    systems = x.shape[0]
    group = ct.shape[0]
    coarse = own // AGGR
    chunks = own // UNROLL
    pieces = own // PIECE
    hbm = pl.BlockSpec(memory_space=pl.ANY)
    smem = pl.BlockSpec(memory_space=pltpu.SMEM)
    block = (systems, width)
    return pl.pallas_call(
        functools.partial(kernel, n, m),
        out_shape=jax.ShapeDtypeStruct(x.shape, F32),
        in_specs=[hbm] * 7 + [smem] * 4,
        out_specs=hbm,
        scratch_shapes=[
            pltpu.VMEM(x.shape, F32),
            pltpu.VMEM(x.shape, F32),
            pltpu.VMEM((own, tiles * width, width), BF),
            pltpu.VMEM((own, width, width), BF),
            pltpu.VMEM((own, width), jnp.int32),
            pltpu.VMEM((coarse, tiles * width, width), BF),
            pltpu.VMEM((coarse, width, width), BF),
            pltpu.VMEM((own,) + block, F32),
            pltpu.VMEM((own,) + block, BF),
            pltpu.VMEM((own,) + block, F32),
            pltpu.VMEM((own, width, width), BF),
            pltpu.VMEM((6, n) + block, BF),
            [pltpu.VMEM((n,) + block, BF)] * 6,
            pltpu.VMEM((coarse,) + block, F32),
            pltpu.VMEM((coarse,) + block, BF),
            pltpu.VMEM((coarse, 2 * systems, width), BF),
            pltpu.VMEM((group,) + block, BF),
            pltpu.SemaphoreType.DMA((6,)),
            pltpu.SemaphoreType.DMA((pieces,)),
            pltpu.SemaphoreType.DMA((6,)),
            pltpu.SemaphoreType.DMA((6,)),
            pltpu.SemaphoreType.DMA((3,)),
            pltpu.SemaphoreType.DMA((3,)),
            pltpu.SemaphoreType.DMA((chunks,)),
        ],
        compiler_params=pltpu.CompilerParams(
            collective_id=0, has_side_effects=True, vmem_limit_bytes=60 * 1024 * 1024
        ),
        cost_estimate=pl.CostEstimate(
            flops=6_000_000_000, bytes_accessed=27_000_000, transcendentals=0
        ),
    )(
        x,
        b,
        ft.reshape(own, tiles * width, width),
        fs,
        amap.reshape(own, width),
        ct.reshape(group, tiles * width, width),
        cs,
        fc.T,
        fsend,
        cc.T,
        csend,
    )


def solution(mesh):
    return jax.shard_map(
        functools.partial(shards, mesh.shape["dom"], mesh.shape["agg"]),
        mesh=mesh,
        in_specs=(
            P(None, ("dom", "agg")),
            P(None, ("dom", "agg")),
            P(("dom", "agg"), None, None, None),
            P(("dom", "agg"), None, None),
            P(("dom", "agg"), None),
            P(("dom", "agg"), None),
            P(("dom", "agg")),
            P("dom", None, None, None),
            P("dom", None, None),
            P("dom", None),
            P("dom", None),
        ),
        out_specs=P(None, ("dom", "agg")),
        check_vma=False,
    )
```

```python
import functools

import jax
import jax.numpy as jnp
from jax import lax
from jax.experimental import pallas as pl
from jax.experimental.pallas import tpu as pltpu
from jax.sharding import PartitionSpec as P

AGGR = 8
LOCAL = 4
BF = jnp.bfloat16
F32 = jnp.float32
MESH = pl.DeviceIdType.MESH
UNROLL = 32
PIECE = 8


def mm(a, b):
    return jnp.dot(a, b, preferred_element_type=F32)


def kernel(
    n,
    m,
    x_in,
    b_in,
    ft_in,
    fs_in,
    map_in,
    ct_in,
    cs_in,
    fc,
    fsend,
    cc,
    csend,
    out,
    stage,
    b,
    ft,
    fs,
    amap,
    ct,
    cs,
    x,
    xb,
    acc,
    member,
    send,
    ghost,
    e1,
    cb,
    e2,
    gath,
    lsem,
    tsem,
    ssem,
    rsem,
    gssem,
    grsem,
    osem,
):
    me = lax.axis_index("dom")
    ag = lax.axis_index("agg")
    own, systems, width = x.shape
    coarse = own // AGGR
    chunks = own // UNROLL
    pieces = own // PIECE
    split = LOCAL * width

    def lanes(r, count=1):
        return pl.ds(pl.multiple_of(r * width, width), count * width)

    load_x = pltpu.make_async_copy(x_in, stage, lsem.at[0])
    load_map = pltpu.make_async_copy(map_in, amap, lsem.at[1])
    load_b = pltpu.make_async_copy(b_in, b, lsem.at[2])
    load_fs = pltpu.make_async_copy(fs_in, fs, lsem.at[3])
    mine = pl.ds(ag * coarse, coarse)
    load_ct = pltpu.make_async_copy(ct_in.at[mine], ct, lsem.at[4])
    load_cs = pltpu.make_async_copy(cs_in.at[mine], cs, lsem.at[5])

    def load_tiles(c):
        rows = pl.ds(c * PIECE, PIECE)
        return pltpu.make_async_copy(ft_in.at[rows], ft.at[rows], tsem.at[c])

    load_x.start()
    load_map.start()
    load_b.start()
    for c in range(pieces):
        load_tiles(c).start()
    load_fs.start()
    load_ct.start()
    load_cs.start()

    barrier = pltpu.get_barrier_semaphore()
    for o in range(1, n):
        pl.semaphore_signal(
            barrier, inc=1, device_id=(lax.rem(me + o, n), ag), device_id_type=MESH
        )
    for o in range(1, m):
        pl.semaphore_signal(
            barrier, inc=1, device_id=(me, lax.rem(ag + o, m)), device_id_type=MESH
        )

    def exchange(e, table, rows_of):
        group = min(PIECE, n)
        for first in range(1, n + 1, group):
            places = [lax.rem(me + o, n) for o in range(first, min(first + group, n + 1))]
            values = rows_of([table[0, d] for d in places])
            for i, (d, value) in enumerate(zip(places, values)):
                if first + i < n:
                    send[e, d] = value
                else:
                    ghost[e][d] = value
            for i, d in enumerate(places):
                if first + i < n:
                    pltpu.make_async_remote_copy(
                        src_ref=send.at[e, d],
                        dst_ref=ghost[e].at[me],
                        send_sem=ssem.at[e],
                        recv_sem=rsem.at[e],
                        device_id=(d, ag),
                        device_id_type=MESH,
                    ).start()

    def all_of(e):
        return pltpu.make_async_remote_copy(
            src_ref=send.at[e, pl.ds(0, n - 1)],
            dst_ref=ghost[e].at[pl.ds(0, n - 1)],
            send_sem=ssem.at[e],
            recv_sem=rsem.at[e],
            device_id=(lax.rem(me + 1, n), ag),
            device_id_type=MESH,
        )

    def ghost_part(e, r):
        near = ft.shape[1] // width
        parts = [ghost[e][jnp.maximum(fc[k, r] - own, 0)] for k in range(LOCAL, near)]
        return mm(jnp.concatenate(parts, axis=1), ft[r, split:, :])

    def local_phase(waits):
        size = PIECE if waits else UNROLL

        @pl.loop(0, own // size)
        def _(c):
            if waits:
                load_tiles(c).wait()
            for u in range(size):
                r = c * size + u
                parts = [xb[r]] + [xb[fc[k, r]] for k in range(1, LOCAL)]
                total = mm(jnp.concatenate(parts, axis=1), ft[r, :split, :])
                acc[r] = b[:, lanes(r)] - total

    def updated(e, rows):
        rest = [(acc[r] - ghost_part(e, r)).astype(BF) for r in rows]
        return [x[r] + mm(v, fs[r]) for r, v in zip(rows, rest)]

    def ghost_phase(e):
        @pl.loop(0, chunks)
        def _(c):
            rows = [c * UNROLL + u for u in range(UNROLL)]
            fresh = updated(e, rows)
            for r, v in zip(rows, fresh):
                x[r] = v
                xb[r] = v.astype(BF)

    def sweep(e, waits=False):
        local_phase(waits)
        if waits:
            load_fs.wait()
        all_of(e).wait_recv()
        exchange(e + 1, fsend, lambda rows: [v.astype(BF) for v in updated(e, rows)])
        ghost_phase(e)

    load_x.wait()

    @pl.loop(0, pieces)
    def _(c):
        for u in range(PIECE):
            r = c * PIECE + u
            v = stage[:, lanes(r)]
            x[r] = v
            xb[r] = v.astype(BF)

    pl.semaphore_wait(barrier, n - 1 + m - 1)
    exchange(0, fsend, lambda rows: [xb[r] for r in rows])

    load_map.wait()

    @pl.loop(0, own, unroll=8)
    def _(r):
        names = amap[pl.ds(r, 1), :] - (r // AGGR) * width
        wanted = lax.broadcasted_iota(jnp.int32, (width, width), 0)
        member[r] = jnp.where(names == wanted, 1.0, 0.0).astype(BF)

    load_b.wait()
    sweep(0, True)
    sweep(1)

    local_phase(False)
    load_ct.wait()
    load_cs.wait()
    all_of(2).wait_recv()

    @pl.loop(0, coarse, unroll=4)
    def _(c):
        rows = [c * AGGR + u for u in range(AGGR)]
        remain = [acc[r] - ghost_part(2, r) for r in rows]
        high = [v.astype(BF) for v in remain]
        low = [(v - h.astype(F32)).astype(BF) for v, h in zip(remain, high)]
        both = jnp.concatenate(
            [jnp.concatenate(high, axis=1), jnp.concatenate(low, axis=1)], axis=0
        )
        table = jnp.concatenate([member[r] for r in rows], axis=1)
        total = lax.dot_general(
            both, table, (((1,), (1,)), ((), ())), preferred_element_type=F32
        )
        kept = (total[:systems] + total[systems:]).astype(BF)
        cb[c] = kept
        first = mm(kept, cs[c])
        e1[c] = first
        gath[ag * coarse + c] = first.astype(BF)

    def slab(owner):
        return pl.ds(owner * coarse, coarse)

    def gather_to(other, owner, slot):
        return pltpu.make_async_remote_copy(
            src_ref=gath.at[slab(owner)],
            dst_ref=gath.at[slab(owner)],
            send_sem=gssem.at[slot],
            recv_sem=grsem.at[slot],
            device_id=(me, other),
            device_id_type=MESH,
        )

    mate = ag + 1 - 2 * lax.rem(ag, 2)
    far = lax.rem(ag + 2, 4)
    gathers = [gather_to(far, ag, 0), gather_to(mate, ag, 1), gather_to(mate, far, 2)]
    gathers[0].start()
    gathers[1].start()
    gathers[0].wait_recv()
    gathers[2].start()
    gathers[1].wait_recv()
    gathers[2].wait_recv()
    exchange(5, csend, lambda rows: [gath[r] for r in rows])
    left = []
    for j in range(coarse):
        r = ag * coarse + j
        parts = [gath[r]] + [gath[cc[k, r]] for k in range(1, LOCAL)]
        left.append(cb[j].astype(F32) - mm(jnp.concatenate(parts, axis=1), ct[j, :split, :]))
    for j in range(coarse):
        acc[j] = left[j]
    all_of(5).wait_recv()
    group = m * coarse
    rest = []
    for j in range(coarse):
        r = ag * coarse + j
        near = ct.shape[1] // width
        parts = [ghost[5][jnp.maximum(cc[k, r] - group, 0)] for k in range(LOCAL, near)]
        rest.append((acc[j] - mm(jnp.concatenate(parts, axis=1), ct[j, split:, :])).astype(BF))
    for j in range(coarse):
        second = e1[j] + mm(rest[j], cs[j])
        high = second.astype(BF)
        e2[j, :systems] = high
        e2[j, systems:] = (second - high.astype(F32)).astype(BF)

    def lifted(rows):
        both = [mm(e2[r // AGGR], member[r]) for r in rows]
        return [x[r] + (v[:systems] + v[systems:]) for r, v in zip(rows, both)]

    exchange(3, fsend, lambda rows: [v.astype(BF) for v in lifted(rows)])

    @pl.loop(0, chunks)
    def _(c):
        rows = [c * UNROLL + u for u in range(UNROLL)]
        fresh = lifted(rows)
        for r, v in zip(rows, fresh):
            x[r] = v
            xb[r] = v.astype(BF)

    sweep(3)
    local_phase(False)
    all_of(4).wait_recv()

    def store_out(c):
        place = lanes(c * UNROLL, UNROLL)
        return pltpu.make_async_copy(stage.at[:, place], out.at[:, place], osem.at[c])

    @pl.loop(0, chunks)
    def _(c):
        rows = [c * UNROLL + u for u in range(UNROLL)]
        fresh = updated(4, rows)
        for r, v in zip(rows, fresh):
            stage[:, lanes(r)] = v
        store_out(c).start()

    for e in range(6):
        all_of(e).wait_send()
    for copy in gathers:
        copy.wait_send()

    @pl.loop(0, chunks)
    def _(c):
        store_out(c).wait()


def shards(n, m, x, b, ft, fs, fc, fsend, amap, ct, cs, cc, csend):
    own, tiles, width, _ = ft.shape
    systems = x.shape[0]
    group = ct.shape[0]
    coarse = own // AGGR
    chunks = own // UNROLL
    pieces = own // PIECE
    hbm = pl.BlockSpec(memory_space=pl.ANY)
    smem = pl.BlockSpec(memory_space=pltpu.SMEM)
    block = (systems, width)
    return pl.pallas_call(
        functools.partial(kernel, n, m),
        out_shape=jax.ShapeDtypeStruct(x.shape, F32),
        in_specs=[hbm] * 7 + [smem] * 4,
        out_specs=hbm,
        scratch_shapes=[
            pltpu.VMEM(x.shape, F32),
            pltpu.VMEM(x.shape, F32),
            pltpu.VMEM((own, tiles * width, width), BF),
            pltpu.VMEM((own, width, width), BF),
            pltpu.VMEM((own, width), jnp.int32),
            pltpu.VMEM((coarse, tiles * width, width), BF),
            pltpu.VMEM((coarse, width, width), BF),
            pltpu.VMEM((own,) + block, F32),
            pltpu.VMEM((own,) + block, BF),
            pltpu.VMEM((own,) + block, F32),
            pltpu.VMEM((own, width, width), BF),
            pltpu.VMEM((6, n) + block, BF),
            [pltpu.VMEM((n,) + block, BF)] * 6,
            pltpu.VMEM((coarse,) + block, F32),
            pltpu.VMEM((coarse,) + block, BF),
            pltpu.VMEM((coarse, 2 * systems, width), BF),
            pltpu.VMEM((group,) + block, BF),
            pltpu.SemaphoreType.DMA((6,)),
            pltpu.SemaphoreType.DMA((pieces,)),
            pltpu.SemaphoreType.DMA((6,)),
            pltpu.SemaphoreType.DMA((6,)),
            pltpu.SemaphoreType.DMA((3,)),
            pltpu.SemaphoreType.DMA((3,)),
            pltpu.SemaphoreType.DMA((chunks,)),
        ],
        compiler_params=pltpu.CompilerParams(
            collective_id=0, has_side_effects=True, vmem_limit_bytes=60 * 1024 * 1024
        ),
        cost_estimate=pl.CostEstimate(
            flops=6_000_000_000, bytes_accessed=27_000_000, transcendentals=0
        ),
    )(
        x,
        b,
        ft.reshape(own, tiles * width, width),
        fs,
        amap.reshape(own, width),
        ct.reshape(group, tiles * width, width),
        cs,
        fc.T,
        fsend,
        cc.T,
        csend,
    )


def solution(mesh):
    return jax.shard_map(
        functools.partial(shards, mesh.shape["dom"], mesh.shape["agg"]),
        mesh=mesh,
        in_specs=(
            P(None, ("dom", "agg")),
            P(None, ("dom", "agg")),
            P(("dom", "agg"), None, None, None),
            P(("dom", "agg"), None, None),
            P(("dom", "agg"), None),
            P(("dom", "agg"), None),
            P(("dom", "agg")),
            P("dom", None, None, None),
            P("dom", None, None),
            P("dom", None),
            P("dom", None),
        ),
        out_specs=P(None, ("dom", "agg")),
        check_vma=False,
    )
```
